32 devices in a mesh: dp: 8 (over z, x), date: 4 (over y, core).
Axes of the slice: x: 2, y: 2, z: 4, core: 2. Of those that a mesh axis runs over, the one named last changes fastest.
Arguments:
- inputs: bfloat16 [8, 16, 32, 512], P('dp', 'date'), may hold values from -6 to 6
- pre_act: bfloat16 [8, 16, 32, 2048], P('dp', 'date'), may hold values from -6 to 6
- hidden_grad: bfloat16 [8, 16, 32, 2048], P('dp', 'date'), may hold values from -6 to 6
- weight_in: bfloat16 [512, 2048], replicated, may hold values from -0.125 to 0.125
- error_in: bfloat16 [8, 512, 2048], P('dp', 'date'), may hold values from -2 to 2, as said below
- q_prev: float32 [2048, 64], replicated, may hold values from -6 to 6
Outputs:
- input_grad: bfloat16 [8, 16, 32, 512], P('dp', None, 'date')
- p_hat: float32 [512, 64], P('date')
- q_new: float32 [2048, 64], replicated
- error_out: bfloat16 [8, 512, 2048], P('dp', 'date')
The draws below stay inside these ranges and needn't reach their ends.
Inputs may be any that keep to these rules, and one draw needn't show every extreme that they name: `error_in`: each group's buffer is a part common to all groups plus a part of its own.
All inputs are finite; a program needn't handle non-finite values.
Results may differ from the reference program's by a relative error of at most 0.005.
Values may be sent and summed in bfloat16 or wider, within the bound.
A program may use at most 64 MiB of HBM per device.

```python
import jax
import jax.numpy as jnp
from jax import lax

DW = 512
HW = 2048
RANK = 64
PATCHES = 32
SAMPLES = 8
DATES = 16
GROUPS = 8
GROUP_TOKENS = 512


def draw_error_in(key, part):
    key = jax.random.fold_in(key, 7)
    shared_key = jax.random.fold_in(key, 1)
    own_key = jax.random.fold_in(key, 2)
    shared = jax.random.normal(shared_key, (1, DW, HW), jnp.float32)
    own = jax.random.normal(own_key, (GROUPS, DW, HW), jnp.float32)
    return jnp.clip(1.2 * shared + 0.6 * own, -2.0, 2.0).astype(jnp.bfloat16)


def steps_of(key, shape, split, low, high):
    gain, own = 1.0, jax.random.fold_in(key, 6)
    for dim, blocks in split:
        draws = jnp.exp(jax.random.uniform(jax.random.fold_in(own, dim), (blocks,), jnp.float32, low / len(split), high / len(split)))
        gain = gain * jnp.repeat(draws, shape[dim] // blocks).reshape([-1 if axis == dim else 1 for axis in range(len(shape))])
    return gain


def gaussian(key, shape, width, limit, cuts=(), dtype=jnp.bfloat16):
    entries = jax.random.normal(key, shape, jnp.float32) * width
    if len(cuts) > 0:
        entries = steps_of(key, shape, cuts, -0.22, 0.18) * entries
    return jnp.clip(entries, min=-limit, max=limit).astype(dtype)


def setup_inputs(seed: int = 0) -> dict:
    keys = jax.random.split(jax.random.key(seed), 7)
    return {
        "inputs": gaussian(keys[0], (SAMPLES, DATES, PATCHES, DW), 1.0, 6.0, ((0, 8), (1, 4))),
        "pre_act": gaussian(keys[1], (SAMPLES, DATES, PATCHES, HW), 1.0, 6.0, ((0, 8), (1, 4))),
        "hidden_grad": gaussian(keys[2], (SAMPLES, DATES, PATCHES, HW), 1.0, 6.0, ((0, 8), (1, 4))),
        "weight_in": gaussian(keys[3], (DW, HW), HW ** -0.5, 0.125),
        "error_in": draw_error_in(jax.random.fold_in(keys[6], 71), 0),
        "q_prev": gaussian(keys[5], (HW, RANK), 1.0, 6.0, (), jnp.float32),
    }


inv_root2 = 0.7071067811865476
inv_root_twopi = 0.3989422804014327
highest = lax.Precision.HIGHEST

def gelu_slope(pre_act):
    value = pre_act.astype(jnp.float32)
    return 0.5 * (1.0 + lax.erf(value * inv_root2)) + value * jnp.exp(-0.5 * value * value) * inv_root_twopi

def reference(inputs, pre_act, hidden_grad, weight_in, error_in, q_prev):
    grad_scale = GROUP_TOKENS ** (-0.5)
    token_rows = inputs.reshape(GROUPS, GROUP_TOKENS, DW)
    pre_rows = pre_act.reshape(GROUPS, GROUP_TOKENS, HW)
    grad_rows = hidden_grad.reshape(GROUPS, GROUP_TOKENS, HW)

    def group_pass(items):
        feats, pres, grads, errors = items
        slope_grad = (grads.astype(jnp.float32) * gelu_slope(pres)).astype(jnp.bfloat16)
        back = lax.dot_general(slope_grad.astype(jnp.float32), weight_in.astype(jnp.float32), (((1,), (1,)), ((), ())), preferred_element_type=jnp.float32).astype(jnp.bfloat16)
        weight_grad = lax.dot_general(feats.astype(jnp.float32), slope_grad.astype(jnp.float32), (((0,), (0,)), ((), ())), preferred_element_type=jnp.float32)
        merged = errors.astype(jnp.float32) + grad_scale * weight_grad
        projected = jnp.dot(merged, q_prev, precision=highest)
        return (back, merged, projected)
    back, merged, projected = lax.map(group_pass, (token_rows, pre_rows, grad_rows, error_in))
    proj = jnp.sum(projected, axis=0)
    gram_matrix = jnp.dot(proj.T, proj, precision=highest)
    factor = jnp.linalg.cholesky(gram_matrix)
    p_hat = jax.scipy.linalg.solve_triangular(factor, proj.T, lower=True).T

    def right_term(matrix):
        return jnp.dot(matrix.T, p_hat, precision=highest)
    q_new = jnp.sum(lax.map(right_term, merged), axis=0) / GROUPS

    def new_error(matrix):
        return (matrix - jnp.dot(p_hat, q_new.T, precision=highest)).astype(jnp.bfloat16)
    error_out = lax.map(new_error, merged)
    input_grad = back.reshape(SAMPLES, DATES, PATCHES, DW)
    return (input_grad, p_hat, q_new, error_out)
```

```python
import functools

import jax
import jax.numpy as jnp
from jax import lax
from jax.experimental import pallas as pl
from jax.experimental.pallas import tpu as pltpu
from jax.sharding import PartitionSpec as P

inv_root2 = 0.7071067811865476
inv_root_twopi = 0.3989422804014327
highest = lax.Precision.HIGHEST
MESH = pl.DeviceIdType.MESH
f32 = jnp.float32
bf16 = jnp.bfloat16


def gelu_slope(pre_act):
    value = pre_act.astype(jnp.float32)
    return (
        0.5 * (1.0 + lax.erf(value * inv_root2))
        + value * jnp.exp(-0.5 * value * value) * inv_root_twopi
    )


def dot(a, b, ca, cb, precision=None):
    return lax.dot_general(
        a, b, (((ca,), (cb,)), ((), ())), preferred_element_type=f32, precision=precision
    )


def parts(value):
    high = value.astype(bf16)
    return high, (value - high.astype(f32)).astype(bf16)


def whiten(proj_t):
    rank = proj_t.shape[0]
    gram = dot(proj_t, proj_t, 1, 1, highest)
    rows = lax.broadcasted_iota(jnp.int32, (rank, rank), 0)
    cols = lax.broadcasted_iota(jnp.int32, (rank, rank), 1)
    eye = (rows == cols).astype(f32)
    table = jnp.concatenate([gram, eye], axis=1)
    blocks = [table[8 * i : 8 * i + 8] for i in range(rank // 8)]
    sub = lax.broadcasted_iota(jnp.int32, (8, 2 * rank), 0)
    for k in range(rank):
        i, r = divmod(k, 8)
        row = blocks[i][r : r + 1, :]
        row = row * (1.0 / row[:, k : k + 1])
        for j in range(i, rank // 8):
            update = blocks[j][:, k : k + 1] * row
            if j == i:
                update = jnp.where(sub > r, update, 0.0)
            blocks[j] = blocks[j] - update
    table = jnp.concatenate(blocks, axis=0)
    pivots = jnp.sum(table[:, :rank] * eye, axis=1, keepdims=True)
    return dot(table[:, rank:] * lax.rsqrt(pivots), proj_t, 1, 0, highest)


def kernel(
    n_dp,
    n_date,
    patches,
    x_hbm,
    pre_hbm,
    hid_hbm,
    w_hbm,
    err_hbm,
    q_hbm,
    ig_ref,
    p_ref,
    qn_ref,
    eo_ref,
    x_v,
    pre_v,
    hid_v,
    w_v,
    stack,
    q_v,
    slopes,
    xcols,
    back_send,
    back_recv,
    proj_part,
    proj_recv,
    proj_full,
    p_full,
    right_send,
    right_recv,
    right_full,
    merged,
    load_sem,
    slope_send,
    slope_recv,
    xcol_send,
    xcol_recv,
    ig_send,
    ig_recv,
    pr_send,
    pr_recv,
    pg_send,
    pg_recv,
    qr_send,
    qr_recv,
    qg_send,
    qg_recv,
):
    tokens, width_in = x_v.shape
    width_hidden = stack.shape[1]
    rank = q_v.shape[1]
    cols_own = width_in // n_date
    scale = (tokens * n_date) ** (-0.5)
    pa = rank // n_dp
    qa, qb = width_hidden // n_dp, rank // n_date
    half = tokens // 2
    dp = lax.axis_index("dp")
    date = lax.axis_index("date")
    others = [(i, j) for i in range(n_dp) for j in range(n_date) if i + j > 0]
    others = sorted(others, key=lambda o: -min(o[0], n_dp - o[0]))

    def slot(o):
        return o[0] * n_date + o[1]

    def target(o):
        return lax.rem(dp + o[0], n_dp), lax.rem(date + o[1], n_date)

    loads = []
    for c in range(2):
        for h, v in ((pre_hbm, pre_v), (hid_hbm, hid_v)):
            rows = pl.ds(c * half, half)
            loads.append((h.at[rows], v.at[rows]))
    loads.append((q_hbm, q_v))
    loads.append((err_hbm, stack.at[pl.ds(tokens, cols_own)]))
    loads.append((x_hbm, x_v))
    loads.append((w_hbm, w_v))
    loads = [pltpu.make_async_copy(s, d, load_sem.at[n]) for n, (s, d) in enumerate(loads)]
    for copy in loads:
        copy.start()

    barrier = pltpu.get_barrier_semaphore()
    for o in others:
        pl.semaphore_signal(barrier, inc=1, device_id=target(o), device_id_type=MESH)

    def remote(src, dst, send, recv, device):
        return pltpu.make_async_remote_copy(
            src_ref=src,
            dst_ref=dst,
            send_sem=send,
            recv_sem=recv,
            device_id=device,
            device_id_type=MESH,
        )

    mate = date + 1 - 2 * lax.rem(date, 2)
    across = lax.rem(date + 2, n_date)
    diag = lax.rem(mate + 2, n_date)
    sent = []

    def slope_copy(c, kind):
        rows = pl.ds(c * half, half)
        src = stack.at[rows] if kind < 2 else slopes.at[1, rows]
        device = (dp, across if kind == 1 else mate)
        n = 2 * kind + c
        return remote(src, slopes.at[kind, rows], slope_send.at[n], slope_recv.at[n], device)

    for c in range(2):
        loads[2 * c].wait()
        loads[2 * c + 1].wait()
        for s in range(half // 16):
            rows = pl.ds(c * half + s * 16, 16)
            stack[rows, :] = (hid_v[rows, :].astype(f32) * gelu_slope(pre_v[rows, :])).astype(bf16)
        if c == 0:
            pl.semaphore_wait(barrier, len(others))
        for kind in (1, 0):
            copy = slope_copy(c, kind)
            copy.start()
            sent.append(copy)

    loads[4].wait()
    loads[5].wait()
    q_high, q_low = parts(q_v[...])
    both = stack[...]
    seen = dot(both, q_high, 1, 0) + dot(both, q_low, 1, 0)
    loads[6].wait()
    x = x_v[...]
    y_high, y_low = parts(seen[:tokens] * scale)
    proj_part[...] = dot(y_high, x, 0, 0) + dot(y_low, x, 0, 0)
    own_cols = pl.ds(pl.multiple_of(date * cols_own, cols_own), cols_own)
    proj_part[:, own_cols] += seen[tokens:].T

    def proj_tile(ref, i, j):
        return ref.at[
            pl.ds(pl.multiple_of(i * pa, pa), pa),
            pl.ds(pl.multiple_of(j * cols_own, cols_own), cols_own),
        ]

    reduce_copies = []
    for o in others:
        n = slot(o)
        to = target(o)
        copy = remote(
            proj_tile(proj_part, *to), proj_recv.at[n], pr_send.at[n], pr_recv.at[n], to
        )
        copy.start()
        reduce_copies.append(copy)
        sent.append(copy)

    x_copies, ig_copies = [], []
    for off in range(1, n_date):
        peer = lax.rem(date + off, n_date)
        cols = pl.ds(pl.multiple_of(peer * cols_own, cols_own), cols_own)
        copy = remote(
            x_v.at[:, cols], xcols.at[off], xcol_send.at[off], xcol_recv.at[off], (dp, peer)
        )
        copy.start()
        x_copies.append(copy)
        sent.append(copy)
    loads[7].wait()
    back = dot(stack[:tokens, :], w_v[...], 1, 1)
    dates = tokens // (patches * n_date)
    for j in range(n_date):
        pieces = [
            back[d * n_date * patches + j * patches : d * n_date * patches + (j + 1) * patches]
            for d in range(dates)
        ]
        back_send[j] = jnp.concatenate(pieces, axis=0).astype(bf16)
    for off in range(1, n_date):
        peer = lax.rem(date + off, n_date)
        copy = remote(
            back_send.at[peer], back_recv.at[off], ig_send.at[off], ig_recv.at[off], (dp, peer)
        )
        copy.start()
        ig_copies.append(copy)
        sent.append(copy)

    total = proj_tile(proj_part, dp, date)[...]
    for o, copy in zip(others, reduce_copies):
        copy.wait_recv()
        total = total + proj_recv[slot(o)]
    mine = proj_tile(proj_full, dp, date)
    mine[...] = total
    for o in others:
        n = slot(o)
        copy = remote(mine, mine, pg_send.at[n], pg_recv.at[n], target(o))
        copy.start()
        sent.append(copy)

    xcol = x_v[:, own_cols]
    merged[...] = stack[tokens:, :].astype(f32) + dot(xcol, stack[:tokens, :], 0, 0) * scale

    for o in others:
        n = slot(o)
        source = (lax.rem(dp - o[0] + n_dp, n_dp), lax.rem(date - o[1] + n_date, n_date))
        tile = proj_tile(proj_full, *source)
        remote(tile, tile, pg_send.at[n], pg_recv.at[n], target(o)).wait_recv()
    p_all = whiten(proj_full[...])
    p_full[...] = p_all
    p_own = p_full[:, own_cols]
    p_ref[...] = p_own
    p_high, p_low = parts(p_all)
    z = (dot(p_high, x, 1, 1) + dot(p_low, x, 1, 1)) * scale
    left_high, left_low = parts(jnp.concatenate([z, p_own], axis=1))
    right = dot(left_high, both, 1, 0) + dot(left_low, both, 1, 0)
    right_send[...] = right.astype(bf16)

    def right_tile(ref, i, j):
        return ref.at[
            pl.ds(pl.multiple_of(j * qb, qb), qb), pl.ds(pl.multiple_of(i * qa, qa), qa)
        ]

    reduce_copies = []
    for o in others:
        n = slot(o)
        to = target(o)
        copy = remote(
            right_tile(right_send, *to), right_recv.at[n], qr_send.at[n], qr_recv.at[n], to
        )
        copy.start()
        reduce_copies.append(copy)
        sent.append(copy)

    for c in range(2):
        slope_copy(c, 1).wait_recv()
        copy = slope_copy(c, 2)
        copy.start()
        sent.append(copy)
    for copy in x_copies:
        copy.wait_recv()

    def add_peer(kind, peer):
        off = lax.rem(date - peer + n_date, n_date)
        return dot(xcols[off], slopes[kind], 0, 0) * scale

    for c in range(2):
        slope_copy(c, 0).wait_recv()
    merged[...] += add_peer(0, mate) + add_peer(1, across)

    total = right_tile(right_send, dp, date)[...].astype(f32)
    for o, copy in zip(others, reduce_copies):
        copy.wait_recv()
        total = total + right_recv[slot(o)].astype(f32)
    mine = right_tile(right_full, dp, date)
    mine[...] = (total * (1.0 / n_dp)).astype(bf16)
    for o in others:
        n = slot(o)
        copy = remote(mine, mine, qg_send.at[n], qg_recv.at[n], target(o))
        copy.start()
        sent.append(copy)

    ig_rows = back_send.shape[1]
    for off, copy in zip(range(1, n_date), ig_copies):
        copy.wait_recv()
        source = lax.rem(date - off + n_date, n_date)
        ig_ref[pl.ds(pl.multiple_of(source * ig_rows, ig_rows), ig_rows), :] = back_recv[off]
    ig_ref[pl.ds(pl.multiple_of(date * ig_rows, ig_rows), ig_rows), :] = back_send[date]
    for c in range(2):
        slope_copy(c, 2).wait_recv()
    merged[...] += add_peer(2, diag)
    own_high, own_low = parts(p_own)

    for o in others:
        n = slot(o)
        source = (lax.rem(dp - o[0] + n_dp, n_dp), lax.rem(date - o[1] + n_date, n_date))
        tile = right_tile(right_full, *source)
        remote(tile, tile, qg_send.at[n], qg_recv.at[n], target(o)).wait_recv()
    q_new = right_full[...]
    qn_ref[...] = q_new
    low_rank = dot(own_high, q_new, 0, 0) + dot(own_low, q_new, 0, 0)
    eo_ref[...] = (merged[...] - low_rank).astype(bf16)
    for copy in sent:
        copy.wait_send()


def fused(n_dp, n_date, inputs, pre_act, hidden_grad, weight_in, error_in, q_prev):
    width_in, width_hidden = weight_in.shape
    rank = q_prev.shape[1]
    x = inputs.reshape(-1, width_in)
    tokens = x.shape[0]
    n = n_dp * n_date
    cols_own = width_in // n_date
    patches = inputs.shape[2] // n_date
    ig_rows = inputs.shape[1] * patches
    any_spec = pl.BlockSpec(memory_space=pl.ANY)
    vmem_spec = pl.BlockSpec(memory_space=pltpu.VMEM)
    dma = pltpu.SemaphoreType.DMA
    qa, qb = width_hidden // n_dp, rank // n_date
    ig, p_t, q_t, eo = pl.pallas_call(
        functools.partial(kernel, n_dp, n_date, patches),
        out_shape=(
            jax.ShapeDtypeStruct((n_date * ig_rows, width_in), bf16),
            jax.ShapeDtypeStruct((rank, cols_own), f32),
            jax.ShapeDtypeStruct((rank, width_hidden), bf16),
            jax.ShapeDtypeStruct((cols_own, width_hidden), bf16),
        ),
        in_specs=[any_spec] * 6,
        out_specs=(vmem_spec,) * 4,
        scratch_shapes=[
            pltpu.VMEM((tokens, width_in), bf16),
            pltpu.VMEM((tokens, width_hidden), bf16),
            pltpu.VMEM((tokens, width_hidden), bf16),
            pltpu.VMEM((width_in, width_hidden), bf16),
            pltpu.VMEM((tokens + cols_own, width_hidden), bf16),
            pltpu.VMEM((width_hidden, rank), f32),
            pltpu.VMEM((3, tokens, width_hidden), bf16),
            pltpu.VMEM((n_date, tokens, cols_own), bf16),
            pltpu.VMEM((n_date, ig_rows, width_in), bf16),
            pltpu.VMEM((n_date, ig_rows, width_in), bf16),
            pltpu.VMEM((rank, width_in), f32),
            pltpu.VMEM((n, rank // n_dp, cols_own), f32),
            pltpu.VMEM((rank, width_in), f32),
            pltpu.VMEM((rank, width_in), f32),
            pltpu.VMEM((rank, width_hidden), bf16),
            pltpu.VMEM((n, qb, qa), bf16),
            pltpu.VMEM((rank, width_hidden), bf16),
            pltpu.VMEM((cols_own, width_hidden), f32),
            dma((8,)),
            dma((6,)),
            dma((6,)),
            dma((n_date,)),
            dma((n_date,)),
            dma((n_date,)),
            dma((n_date,)),
        ]
        + [dma((n,))] * 8,
        compiler_params=pltpu.CompilerParams(
            collective_id=0, has_side_effects=True, vmem_limit_bytes=48 * 1024 * 1024
        ),
    )(
        x,
        pre_act.reshape(tokens, width_hidden),
        hidden_grad.reshape(tokens, width_hidden),
        weight_in,
        error_in[0],
        q_prev,
    )
    input_grad = ig.reshape(1, -1, patches, width_in)
    return (input_grad, p_t.T, q_t.astype(f32).T, eo[None])


def orthonormal(proj, gram_matrix):
    factor = jnp.linalg.cholesky(gram_matrix)
    return jax.scipy.linalg.solve_triangular(factor, proj.T, lower=True).T


def staged(inputs, pre_act, hidden_grad, weight_in, error_in, q_prev):
    date_count = lax.axis_size("date")
    width_in = inputs.shape[-1]
    width_hidden = pre_act.shape[-1]
    token_rows = inputs.reshape(-1, width_in)
    grad_scale = (token_rows.shape[0] * date_count) ** (-0.5)
    slope_grad = (
        hidden_grad.reshape(-1, width_hidden).astype(jnp.float32)
        * gelu_slope(pre_act.reshape(-1, width_hidden))
    ).astype(jnp.bfloat16)
    local_back = lax.dot_general(
        slope_grad, weight_in, (((1,), (1,)), ((), ())), preferred_element_type=jnp.float32
    ).astype(jnp.bfloat16)
    input_grad = lax.all_to_all(
        local_back.reshape(inputs.shape), "date", split_axis=2, concat_axis=1, tiled=True
    )
    column_block = lax.all_to_all(token_rows, "date", split_axis=1, concat_axis=0, tiled=True)
    own_grad = grad_scale * lax.dot_general(
        column_block,
        lax.all_gather(slope_grad, "date", axis=0, tiled=True),
        (((0,), (0,)), ((), ())),
        preferred_element_type=jnp.float32,
    )
    own_error = error_in[0].astype(jnp.float32)
    merged_rows = own_error + own_grad
    proj_rows = lax.psum(jnp.dot(merged_rows, q_prev, precision=highest), "dp")
    gram_matrix = lax.psum(jnp.dot(proj_rows.T, proj_rows, precision=highest), "date")
    p_rows = orthonormal(proj_rows, gram_matrix)
    right_part = jnp.dot(merged_rows.T, p_rows, precision=highest)
    q_new = lax.psum(right_part, ("dp", "date")) / lax.axis_size("dp")
    error_out = (merged_rows - jnp.dot(p_rows, q_new.T, precision=highest)).astype(jnp.bfloat16)[
        None
    ]
    return (input_grad, p_rows, q_new, error_out)


def solution(mesh):
    in_specs = (
        P("dp", "date", None, None),
        P("dp", "date", None, None),
        P("dp", "date", None, None),
        P(),
        P("dp", "date", None),
        P(),
    )
    out_specs = (P("dp", None, "date", None), P("date", None), P(), P("dp", "date", None))
    n_dp, n_date = mesh.shape["dp"], mesh.shape["date"]

    def local(*args):
        width_in, width_hidden = args[3].shape
        rank = args[5].shape[1]
        direct = (
            n_date == 4
            and n_dp * n_date <= 64
            and args[0].shape[0] == 1
            and rank % (8 * n_dp) == 0
            and rank % (16 * n_date) == 0
            and width_in % (128 * n_date) == 0
            and width_hidden % (128 * n_dp) == 0
            and args[0].shape[2] % (8 * n_date) == 0
        )
        if direct:
            return fused(n_dp, n_date, *args)
        return staged(*args)

    return jax.shard_map(local, mesh=mesh, in_specs=in_specs, out_specs=out_specs, check_vma=False)
```

```python
import functools

import jax
import jax.numpy as jnp
from jax import lax
from jax.experimental import pallas as pl
from jax.experimental.pallas import tpu as pltpu
from jax.sharding import PartitionSpec as P

panel = 8
inv_root2 = 0.7071067811865476
inv_root_twopi = 0.3989422804014327
highest = lax.Precision.HIGHEST
MESH = pl.DeviceIdType.MESH
f32 = jnp.float32
bf16 = jnp.bfloat16


def gelu_slope(pre_act):
    value = pre_act.astype(jnp.float32)
    return (
        0.5 * (1.0 + lax.erf(value * inv_root2))
        + value * jnp.exp(-0.5 * value * value) * inv_root_twopi
    )


def dot(a, b, ca, cb, precision=None):
    return lax.dot_general(
        a, b, (((ca,), (cb,)), ((), ())), preferred_element_type=f32, precision=precision
    )


def parts(value):
    high = value.astype(bf16)
    return high, (value - high.astype(f32)).astype(bf16)


def whiten(proj_t):
    rank = proj_t.shape[0]
    gram = dot(proj_t, proj_t, 1, 1, highest)
    rows = lax.broadcasted_iota(jnp.int32, (rank, rank), 0)
    cols = lax.broadcasted_iota(jnp.int32, (rank, rank), 1)
    eye = (rows == cols).astype(f32)
    table = jnp.concatenate([gram, eye], axis=1)
    blocks = [table[8 * i : 8 * i + 8] for i in range(rank // 8)]
    sub = lax.broadcasted_iota(jnp.int32, (8, 2 * rank), 0)
    for k in range(0, rank, panel):
        i = k // 8
        cols = {
            j: [jnp.broadcast_to(blocks[j][:, k + m : k + m + 1], sub.shape) for m in range(panel)]
            for j in range(i, rank // 8)
        }
        for m in range(panel):
            r = (k + m) % 8
            row = blocks[i][r : r + 1, :]
            inverse = 1.0 / cols[i][m][r : r + 1, :]
            heads = [cols[i][n][r : r + 1, :] for n in range(panel)]
            for j in range(i, rank // 8):
                factor = cols[j][m] * inverse
                if j == i:
                    factor = jnp.where(sub > r, factor, 0.0)
                for n in range(m + 1, panel):
                    cols[j][n] = cols[j][n] - factor * heads[n]
                blocks[j] = blocks[j] - factor * row
    table = jnp.concatenate(blocks, axis=0)
    pivots = jnp.sum(table[:, :rank] * eye, axis=1, keepdims=True)
    return dot(table[:, rank:] * lax.rsqrt(pivots), proj_t, 1, 0, highest)


def kernel(
    n_dp,
    n_date,
    patches,
    x_hbm,
    pre_hbm,
    hid_hbm,
    w_hbm,
    err_hbm,
    q_hbm,
    ig_out,
    p_out,
    qn_out,
    merged_out,
    x_v,
    pre_v,
    hid_v,
    w_v,
    stack,
    q_v,
    slopes,
    xcols,
    back_send,
    back_recv,
    proj_part,
    proj_recv,
    proj_full,
    p_full,
    right_send,
    right_recv,
    right_full,
    merged,
    ig_ref,
    load_sem,
    store_sem,
    slope_send,
    slope_recv,
    xcol_send,
    xcol_recv,
    ig_send,
    ig_recv,
    pr_send,
    pr_recv,
    pg_send,
    pg_recv,
    qr_send,
    qr_recv,
    qg_send,
    qg_recv,
):
    tokens, width_in = x_v.shape
    width_hidden = stack.shape[1]
    rank = q_v.shape[0]
    cols_own = width_in // n_date
    scale = (tokens * n_date) ** (-0.5)
    pa = rank // n_dp
    qa, qb = width_hidden // n_dp, rank // n_date
    half = tokens // 2
    dp = lax.axis_index("dp")
    date = lax.axis_index("date")
    others = [(i, j) for i in range(n_dp) for j in range(n_date) if i + j > 0]
    others = sorted(others, key=lambda o: -min(o[0], n_dp - o[0]))

    def slot(o):
        return o[0] * n_date + o[1]

    def target(o):
        return lax.rem(dp + o[0], n_dp), lax.rem(date + o[1], n_date)

    loads = []
    for c in range(2):
        for h, v in ((pre_hbm, pre_v), (hid_hbm, hid_v)):
            rows = pl.ds(c * half, half)
            loads.append((h.at[rows], v.at[rows]))
    loads.append((q_hbm, q_v))
    loads.append((err_hbm, stack.at[pl.ds(tokens, cols_own)]))
    loads.append((x_hbm, x_v))
    loads.append((w_hbm, w_v))
    loads = [pltpu.make_async_copy(s, d, load_sem.at[n]) for n, (s, d) in enumerate(loads)]
    for copy in loads:
        copy.start()

    barrier = pltpu.get_barrier_semaphore()
    for o in others:
        pl.semaphore_signal(barrier, inc=1, device_id=target(o), device_id_type=MESH)

    def remote(src, dst, send, recv, device):
        return pltpu.make_async_remote_copy(
            src_ref=src,
            dst_ref=dst,
            send_sem=send,
            recv_sem=recv,
            device_id=device,
            device_id_type=MESH,
        )

    mate = date + 1 - 2 * lax.rem(date, 2)
    across = lax.rem(date + 2, n_date)
    diag = lax.rem(mate + 2, n_date)
    sent = []

    def slope_copy(c, kind):
        rows = pl.ds(c * half, half)
        src = stack.at[rows] if kind < 2 else slopes.at[1, rows]
        device = (dp, across if kind == 1 else mate)
        n = 2 * kind + c
        return remote(src, slopes.at[kind, rows], slope_send.at[n], slope_recv.at[n], device)

    for c in range(2):
        loads[2 * c].wait()
        loads[2 * c + 1].wait()
        for s in range(half // 16):
            rows = pl.ds(c * half + s * 16, 16)
            stack[rows, :] = (hid_v[rows, :].astype(f32) * gelu_slope(pre_v[rows, :])).astype(bf16)
        if c == 0:
            pl.semaphore_wait(barrier, len(others))
        for kind in (1, 0) if c == 0 else (0,):
            copy = slope_copy(c, kind)
            copy.start()
            sent.append(copy)

    loads[4].wait()
    loads[5].wait()
    q_high, q_low = parts(q_v[...])
    both = stack[...]
    seen = dot(q_high, both, 1, 1) + dot(q_low, both, 1, 1)
    loads[6].wait()
    x = x_v[...]
    y_high, y_low = parts(seen[:, :tokens] * scale)
    proj_part[...] = dot(y_high, x, 1, 0) + dot(y_low, x, 1, 0)
    own_cols = pl.ds(pl.multiple_of(date * cols_own, cols_own), cols_own)
    proj_part[:, own_cols] += seen[:, tokens:]

    def proj_tile(ref, i, j):
        return ref.at[
            pl.ds(pl.multiple_of(i * pa, pa), pa),
            pl.ds(pl.multiple_of(j * cols_own, cols_own), cols_own),
        ]

    reduce_copies = []
    for o in others:
        n = slot(o)
        to = target(o)
        copy = remote(
            proj_tile(proj_part, *to), proj_recv.at[n], pr_send.at[n], pr_recv.at[n], to
        )
        copy.start()
        reduce_copies.append(copy)
        sent.append(copy)

    x_copies, ig_copies = [], []
    for off in range(1, n_date):
        peer = lax.rem(date + off, n_date)
        cols = pl.ds(pl.multiple_of(peer * cols_own, cols_own), cols_own)
        copy = remote(
            x_v.at[:, cols], xcols.at[off], xcol_send.at[off], xcol_recv.at[off], (dp, peer)
        )
        copy.start()
        x_copies.append(copy)
        sent.append(copy)
    loads[7].wait()
    back = dot(stack[:tokens, :], w_v[...], 1, 1)
    dates = tokens // (patches * n_date)
    for j in range(n_date):
        pieces = [
            back[d * n_date * patches + j * patches : d * n_date * patches + (j + 1) * patches]
            for d in range(dates)
        ]
        back_send[j] = jnp.concatenate(pieces, axis=0).astype(bf16)
    for off in range(1, n_date):
        peer = lax.rem(date + off, n_date)
        copy = remote(
            back_send.at[peer], back_recv.at[off], ig_send.at[off], ig_recv.at[off], (dp, peer)
        )
        copy.start()
        ig_copies.append(copy)
        sent.append(copy)

    total = proj_tile(proj_part, dp, date)[...]
    for o, copy in zip(others, reduce_copies):
        copy.wait_recv()
        total = total + proj_recv[slot(o)]
    mine = proj_tile(proj_full, dp, date)
    mine[...] = total
    for o in others:
        n = slot(o)
        copy = remote(mine, mine, pg_send.at[n], pg_recv.at[n], target(o))
        copy.start()
        sent.append(copy)

    xcol = x_v[:, own_cols]
    merged[...] = stack[tokens:, :].astype(f32) + dot(xcol, stack[:tokens, :], 0, 0) * scale

    for o in others:
        n = slot(o)
        source = (lax.rem(dp - o[0] + n_dp, n_dp), lax.rem(date - o[1] + n_date, n_date))
        tile = proj_tile(proj_full, *source)
        remote(tile, tile, pg_send.at[n], pg_recv.at[n], target(o)).wait_recv()
    copy = slope_copy(1, 1)
    copy.start()
    sent.append(copy)
    p_all = whiten(proj_full[...])
    p_full[...] = p_all
    p_own = p_full[:, own_cols]
    stores = [pltpu.make_async_copy(p_full.at[:, own_cols], p_out, store_sem.at[0])]
    stores[0].start()
    p_high, p_low = parts(p_all)
    z = (dot(p_high, x, 1, 1) + dot(p_low, x, 1, 1)) * scale
    left_high, left_low = parts(jnp.concatenate([z, p_own], axis=1))
    right = dot(left_high, both, 1, 0) + dot(left_low, both, 1, 0)
    right_send[...] = right.astype(bf16)

    def right_tile(ref, i, j):
        return ref.at[
            pl.ds(pl.multiple_of(j * qb, qb), qb), pl.ds(pl.multiple_of(i * qa, qa), qa)
        ]

    reduce_copies = []
    for o in others:
        n = slot(o)
        to = target(o)
        copy = remote(
            right_tile(right_send, *to), right_recv.at[n], qr_send.at[n], qr_recv.at[n], to
        )
        copy.start()
        reduce_copies.append(copy)
        sent.append(copy)

    for c in range(2):
        slope_copy(c, 1).wait_recv()
        copy = slope_copy(c, 2)
        copy.start()
        sent.append(copy)
    for copy in x_copies:
        copy.wait_recv()

    def add_peer(kind, peer):
        off = lax.rem(date - peer + n_date, n_date)
        return dot(xcols[off], slopes[kind], 0, 0) * scale

    for c in range(2):
        slope_copy(c, 0).wait_recv()
    merged[...] += add_peer(0, mate) + add_peer(1, across)

    total = right_tile(right_send, dp, date)[...].astype(f32)
    for o, copy in zip(others, reduce_copies):
        copy.wait_recv()
        total = total + right_recv[slot(o)].astype(f32)
    mine = right_tile(right_full, dp, date)
    mine[...] = (total * (1.0 / n_dp)).astype(bf16)
    for o in others:
        n = slot(o)
        copy = remote(mine, mine, qg_send.at[n], qg_recv.at[n], target(o))
        copy.start()
        sent.append(copy)

    ig_rows = back_send.shape[1]
    for off, copy in zip(range(1, n_date), ig_copies):
        copy.wait_recv()
        source = lax.rem(date - off + n_date, n_date)
        ig_ref[pl.ds(pl.multiple_of(source * ig_rows, ig_rows), ig_rows), :] = back_recv[off]
    ig_ref[pl.ds(pl.multiple_of(date * ig_rows, ig_rows), ig_rows), :] = back_send[date]
    for c in range(2):
        slope_copy(c, 2).wait_recv()
    merged[...] += add_peer(2, diag)
    stores.append(pltpu.make_async_copy(ig_ref, ig_out, store_sem.at[1]))
    stores.append(pltpu.make_async_copy(merged, merged_out, store_sem.at[2]))
    stores[1].start()
    stores[2].start()

    for o in others:
        n = slot(o)
        source = (lax.rem(dp - o[0] + n_dp, n_dp), lax.rem(date - o[1] + n_date, n_date))
        tile = right_tile(right_full, *source)
        remote(tile, tile, qg_send.at[n], qg_recv.at[n], target(o)).wait_recv()
    stores.append(pltpu.make_async_copy(right_full, qn_out, store_sem.at[3]))
    stores[3].start()
    for copy in stores:
        copy.wait()
    for copy in sent:
        copy.wait_send()


def finish(
    ig_hbm, p_hbm, q_hbm, merged_hbm, ig_out, p_out, q_out, eo_out, ig_v, p_v, q_v, wide_v,
    merged_v, eo_v, load_sem, store_sem
):
    rows = merged_v.shape[0] // 4
    cuts = [pl.ds(c * rows, rows) for c in range(4)]
    pairs = [(p_hbm, p_v), (q_hbm, q_v)]
    pairs += [(merged_hbm.at[cut], merged_v.at[cut]) for cut in cuts]
    pairs += [(ig_hbm, ig_v)]
    loads = [pltpu.make_async_copy(s, d, load_sem.at[n]) for n, (s, d) in enumerate(pairs)]
    for copy in loads:
        copy.start()
    pairs = [(p_v, p_out), (wide_v, q_out)]
    pairs += [(eo_v.at[cut], eo_out.at[cut]) for cut in cuts]
    pairs += [(ig_v, ig_out)]
    stores = [pltpu.make_async_copy(s, d, store_sem.at[n]) for n, (s, d) in enumerate(pairs)]
    loads[0].wait()
    stores[0].start()
    loads[1].wait()
    wide_v[...] = q_v[...].astype(f32)
    stores[1].start()
    p_high, p_low = parts(p_v[...])
    for c, cut in enumerate(cuts):
        loads[2 + c].wait()
        p_rows = slice(c * rows, (c + 1) * rows)
        low_rank = dot(p_high[:, p_rows], q_v[...], 0, 0) + dot(p_low[:, p_rows], q_v[...], 0, 0)
        eo_v[cut, :] = (merged_v[cut, :] - low_rank).astype(bf16)
        stores[2 + c].start()
    loads[6].wait()
    stores[6].start()
    for copy in stores:
        copy.wait()


def fused(n_dp, n_date, inputs, pre_act, hidden_grad, weight_in, error_in, q_prev):
    width_in, width_hidden = weight_in.shape
    rank = q_prev.shape[1]
    x = inputs.reshape(-1, width_in)
    tokens = x.shape[0]
    n = n_dp * n_date
    cols_own = width_in // n_date
    patches = inputs.shape[2] // n_date
    ig_rows = inputs.shape[1] * patches
    hbm_spec = pl.BlockSpec(memory_space=pltpu.HBM)
    dma = pltpu.SemaphoreType.DMA
    qa, qb = width_hidden // n_dp, rank // n_date
    ig, p_t, q_t, merged = pl.pallas_call(
        functools.partial(kernel, n_dp, n_date, patches),
        out_shape=(
            jax.ShapeDtypeStruct((n_date * ig_rows, width_in), bf16),
            jax.ShapeDtypeStruct((rank, cols_own), f32),
            jax.ShapeDtypeStruct((rank, width_hidden), bf16),
            jax.ShapeDtypeStruct((cols_own, width_hidden), f32),
        ),
        in_specs=[hbm_spec] * 6,
        out_specs=(hbm_spec,) * 4,
        scratch_shapes=[
            pltpu.VMEM((tokens, width_in), bf16),
            pltpu.VMEM((tokens, width_hidden), bf16),
            pltpu.VMEM((tokens, width_hidden), bf16),
            pltpu.VMEM((width_in, width_hidden), bf16),
            pltpu.VMEM((tokens + cols_own, width_hidden), bf16),
            pltpu.VMEM((rank, width_hidden), f32),
            pltpu.VMEM((3, tokens, width_hidden), bf16),
            pltpu.VMEM((n_date, tokens, cols_own), bf16),
            pltpu.VMEM((n_date, ig_rows, width_in), bf16),
            pltpu.VMEM((n_date, ig_rows, width_in), bf16),
            pltpu.VMEM((rank, width_in), f32),
            pltpu.VMEM((n, rank // n_dp, cols_own), f32),
            pltpu.VMEM((rank, width_in), f32),
            pltpu.VMEM((rank, width_in), f32),
            pltpu.VMEM((rank, width_hidden), bf16),
            pltpu.VMEM((n, qb, qa), bf16),
            pltpu.VMEM((rank, width_hidden), bf16),
            pltpu.VMEM((cols_own, width_hidden), f32),
            pltpu.VMEM((n_date * ig_rows, width_in), bf16),
            dma((8,)),
            dma((4,)),
            dma((6,)),
            dma((6,)),
            dma((n_date,)),
            dma((n_date,)),
            dma((n_date,)),
            dma((n_date,)),
        ]
        + [dma((n,))] * 8,
        compiler_params=pltpu.CompilerParams(
            collective_id=0, has_side_effects=True, vmem_limit_bytes=64 * 1024 * 1024
        ),
    )(
        x,
        pre_act.reshape(tokens, width_hidden),
        hidden_grad.reshape(tokens, width_hidden),
        weight_in,
        error_in[0],
        q_prev.T,
    )
    ig, p_t, q_t, error_out = pl.pallas_call(
        finish,
        out_shape=(
            jax.ShapeDtypeStruct(ig.shape, bf16),
            jax.ShapeDtypeStruct(p_t.shape, f32),
            jax.ShapeDtypeStruct(q_t.shape, f32),
            jax.ShapeDtypeStruct(merged.shape, bf16),
        ),
        in_specs=[hbm_spec] * 4,
        out_specs=(hbm_spec,) * 4,
        scratch_shapes=[
            pltpu.VMEM(ig.shape, bf16),
            pltpu.VMEM(p_t.shape, f32),
            pltpu.VMEM(q_t.shape, bf16),
            pltpu.VMEM(q_t.shape, f32),
            pltpu.VMEM(merged.shape, f32),
            pltpu.VMEM(merged.shape, bf16),
            dma((7,)),
            dma((7,)),
        ],
        compiler_params=pltpu.CompilerParams(vmem_limit_bytes=64 * 1024 * 1024),
    )(ig, p_t, q_t, merged)
    input_grad = ig.reshape(1, -1, patches, width_in)
    return (input_grad, p_t.T, q_t.T, error_out[None])


def orthonormal(proj, gram_matrix):
    factor = jnp.linalg.cholesky(gram_matrix)
    return jax.scipy.linalg.solve_triangular(factor, proj.T, lower=True).T


def staged(inputs, pre_act, hidden_grad, weight_in, error_in, q_prev):
    date_count = lax.axis_size("date")
    width_in = inputs.shape[-1]
    width_hidden = pre_act.shape[-1]
    token_rows = inputs.reshape(-1, width_in)
    grad_scale = (token_rows.shape[0] * date_count) ** (-0.5)
    slope_grad = (
        hidden_grad.reshape(-1, width_hidden).astype(jnp.float32)
        * gelu_slope(pre_act.reshape(-1, width_hidden))
    ).astype(jnp.bfloat16)
    local_back = lax.dot_general(
        slope_grad, weight_in, (((1,), (1,)), ((), ())), preferred_element_type=jnp.float32
    ).astype(jnp.bfloat16)
    input_grad = lax.all_to_all(
        local_back.reshape(inputs.shape), "date", split_axis=2, concat_axis=1, tiled=True
    )
    column_block = lax.all_to_all(token_rows, "date", split_axis=1, concat_axis=0, tiled=True)
    own_grad = grad_scale * lax.dot_general(
        column_block,
        lax.all_gather(slope_grad, "date", axis=0, tiled=True),
        (((0,), (0,)), ((), ())),
        preferred_element_type=jnp.float32,
    )
    own_error = error_in[0].astype(jnp.float32)
    merged_rows = own_error + own_grad
    proj_rows = lax.psum(jnp.dot(merged_rows, q_prev, precision=highest), "dp")
    gram_matrix = lax.psum(jnp.dot(proj_rows.T, proj_rows, precision=highest), "date")
    p_rows = orthonormal(proj_rows, gram_matrix)
    right_part = jnp.dot(merged_rows.T, p_rows, precision=highest)
    q_new = lax.psum(right_part, ("dp", "date")) / lax.axis_size("dp")
    error_out = (merged_rows - jnp.dot(p_rows, q_new.T, precision=highest)).astype(jnp.bfloat16)[
        None
    ]
    return (input_grad, p_rows, q_new, error_out)


def solution(mesh):
    in_specs = (
        P("dp", "date", None, None),
        P("dp", "date", None, None),
        P("dp", "date", None, None),
        P(),
        P("dp", "date", None),
        P(),
    )
    out_specs = (P("dp", None, "date", None), P("date", None), P(), P("dp", "date", None))
    n_dp, n_date = mesh.shape["dp"], mesh.shape["date"]

    def local(*args):
        width_in, width_hidden = args[3].shape
        rank = args[5].shape[1]
        direct = (
            n_date == 4
            and n_dp * n_date <= 64
            and args[0].shape[0] == 1
            and rank % (8 * n_dp) == 0
            and rank % (16 * n_date) == 0
            and width_in % (128 * n_date) == 0
            and width_hidden % (128 * n_dp) == 0
            and args[0].shape[2] % (8 * n_date) == 0
        )
        if direct:
            return fused(n_dp, n_date, *args)
        return staged(*args)

    return jax.shard_map(local, mesh=mesh, in_specs=in_specs, out_specs=out_specs, check_vma=False)
```

```python
import functools

import jax
import jax.numpy as jnp
from jax import lax
from jax.experimental import pallas as pl
from jax.experimental.pallas import tpu as pltpu
from jax.sharding import PartitionSpec as P

panel = 8
inv_root2 = 0.7071067811865476
inv_root_twopi = 0.3989422804014327
highest = lax.Precision.HIGHEST
MESH = pl.DeviceIdType.MESH
f32 = jnp.float32
bf16 = jnp.bfloat16


def gelu_slope(pre_act):
    value = pre_act.astype(jnp.float32)
    return (
        0.5 * (1.0 + lax.erf(value * inv_root2))
        + value * jnp.exp(-0.5 * value * value) * inv_root_twopi
    )


def dot(a, b, ca, cb, precision=None):
    return lax.dot_general(
        a, b, (((ca,), (cb,)), ((), ())), preferred_element_type=f32, precision=precision
    )


def parts(value):
    high = value.astype(bf16)
    return high, (value - high.astype(f32)).astype(bf16)


def whiten(proj_t):
    rank = proj_t.shape[0]
    gram = dot(proj_t, proj_t, 1, 1, highest)
    rows = lax.broadcasted_iota(jnp.int32, (rank, rank), 0)
    cols = lax.broadcasted_iota(jnp.int32, (rank, rank), 1)
    eye = (rows == cols).astype(f32)
    table = jnp.concatenate([gram, eye], axis=1)
    blocks = [table[8 * i : 8 * i + 8] for i in range(rank // 8)]
    sub = lax.broadcasted_iota(jnp.int32, (8, 2 * rank), 0)
    for k in range(0, rank, panel):
        i = k // 8
        cols = {
            j: [jnp.broadcast_to(blocks[j][:, k + m : k + m + 1], sub.shape) for m in range(panel)]
            for j in range(i, rank // 8)
        }
        for m in range(panel):
            r = (k + m) % 8
            row = blocks[i][r : r + 1, :]
            inverse = 1.0 / cols[i][m][r : r + 1, :]
            heads = [cols[i][n][r : r + 1, :] for n in range(panel)]
            for j in range(i, rank // 8):
                factor = cols[j][m] * inverse
                if j == i:
                    factor = jnp.where(sub > r, factor, 0.0)
                for n in range(m + 1, panel):
                    cols[j][n] = cols[j][n] - factor * heads[n]
                blocks[j] = blocks[j] - factor * row
    table = jnp.concatenate(blocks, axis=0)
    pivots = jnp.sum(table[:, :rank] * eye, axis=1, keepdims=True)
    return dot(table[:, rank:] * lax.rsqrt(pivots), proj_t, 1, 0, highest)


def kernel(
    n_dp,
    n_date,
    patches,
    x_hbm,
    pre_hbm,
    hid_hbm,
    w_hbm,
    err_hbm,
    q_hbm,
    ig_out,
    p_out,
    qn_out,
    merged_out,
    x_v,
    pre_v,
    hid_v,
    w_v,
    stack,
    q_v,
    slopes,
    xcols,
    back_send,
    back_recv,
    proj_part,
    proj_recv,
    proj_full,
    p_full,
    right_send,
    right_recv,
    right_full,
    merged,
    ig_ref,
    proj_swap,
    proj_half,
    right_all,
    right_swap,
    right_sum,
    right_half,
    load_sem,
    store_sem,
    swap_send,
    swap_recv,
    slope_send,
    slope_recv,
    xcol_send,
    xcol_recv,
    ig_send,
    ig_recv,
    pr_send,
    pr_recv,
    pg_send,
    pg_recv,
    qr_send,
    qr_recv,
    qg_send,
    qg_recv,
):
    tokens, width_in = x_v.shape
    width_hidden = stack.shape[1]
    rank = q_v.shape[0]
    cols_own = width_in // n_date
    scale = (tokens * n_date) ** (-0.5)
    pa = rank // n_dp
    qa, qb = width_hidden // n_dp, rank // n_date
    half = tokens // 2
    dp = lax.axis_index("dp")
    date = lax.axis_index("date")
    others = [(i, j) for i in range(n_dp) for j in range(n_date) if i + j > 0]
    others = sorted(others, key=lambda o: -min(o[0], n_dp - o[0]))
    same_core = [o for o in others if o[1] % 2 == 0]
    proj_to = others
    right_to = same_core
    core = lax.rem(date, 2)
    chips = n_date // 2

    def place(j):
        return lax.rem(j, 2) * chips + lax.div(j, 2)

    def slot(o):
        return o[0] * n_date + o[1]

    def target(o):
        return lax.rem(dp + o[0], n_dp), lax.rem(date + o[1], n_date)

    loads = []
    for c in range(2):
        for h, v in ((pre_hbm, pre_v), (hid_hbm, hid_v)):
            rows = pl.ds(c * half, half)
            loads.append((h.at[rows], v.at[rows]))
    loads.append((q_hbm, q_v))
    loads.append((err_hbm, stack.at[pl.ds(tokens, cols_own)]))
    loads.append((x_hbm, x_v))
    loads.append((w_hbm, w_v))
    loads = [pltpu.make_async_copy(s, d, load_sem.at[n]) for n, (s, d) in enumerate(loads)]
    for copy in loads:
        copy.start()

    barrier = pltpu.get_barrier_semaphore()
    for o in others:
        pl.semaphore_signal(barrier, inc=1, device_id=target(o), device_id_type=MESH)

    def remote(src, dst, send, recv, device):
        return pltpu.make_async_remote_copy(
            src_ref=src,
            dst_ref=dst,
            send_sem=send,
            recv_sem=recv,
            device_id=device,
            device_id_type=MESH,
        )

    mate = date + 1 - 2 * lax.rem(date, 2)
    across = lax.rem(date + 2, n_date)
    diag = lax.rem(mate + 2, n_date)
    sent = []

    def slope_copy(c, kind):
        rows = pl.ds(c * half, half)
        src = stack.at[rows] if kind < 2 else slopes.at[1, rows]
        device = (dp, across if kind == 1 else mate)
        n = 2 * kind + c
        return remote(src, slopes.at[kind, rows], slope_send.at[n], slope_recv.at[n], device)

    for c in range(2):
        loads[2 * c].wait()
        loads[2 * c + 1].wait()
        for s in range(half // 16):
            rows = pl.ds(c * half + s * 16, 16)
            stack[rows, :] = (hid_v[rows, :].astype(f32) * gelu_slope(pre_v[rows, :])).astype(bf16)
        if c == 0:
            pl.semaphore_wait(barrier, len(others))
        for kind in (1, 0) if c == 0 else (0,):
            copy = slope_copy(c, kind)
            copy.start()
            sent.append(copy)

    loads[4].wait()
    loads[5].wait()
    q_high, q_low = parts(q_v[...])
    both = stack[...]
    seen = dot(q_high, both, 1, 1) + dot(q_low, both, 1, 1)
    loads[6].wait()
    x = x_v[...]
    y_high, y_low = parts(seen[:, :tokens] * scale)
    part = dot(y_high, x, 1, 0) + dot(y_low, x, 1, 0)
    for j in range(n_date):
        proj_part[j % 2 * chips + j // 2] = part[:, j * cols_own : (j + 1) * cols_own]
    proj_part[place(date)] += seen[:, tokens:]

    own_cols = pl.ds(pl.multiple_of(date * cols_own, cols_own), cols_own)
    my_blocks = pl.ds(core * chips, chips)
    mate_blocks = pl.ds((1 - core) * chips, chips)
    swap = remote(
        proj_part.at[mate_blocks], proj_swap, swap_send.at[0], swap_recv.at[0], (dp, mate)
    )
    swap.start()
    sent.append(swap)
    swap.wait_recv()
    proj_half[...] = proj_part[my_blocks] + proj_swap[...]

    def proj_rows(i):
        return pl.ds(pl.multiple_of(i * pa, pa), pa)

    def half_tile(i, j):
        return proj_half.at[lax.div(j, 2), proj_rows(i)]

    def proj_tile(i, j):
        return proj_full.at[place(j), proj_rows(i)]

    reduce_copies = []
    for o in same_core:
        n = slot(o)
        to = target(o)
        copy = remote(half_tile(*to), proj_recv.at[n], pr_send.at[n], pr_recv.at[n], to)
        copy.start()
        reduce_copies.append(copy)
        sent.append(copy)

    x_copies, ig_copies = [], []
    for off in range(1, n_date):
        peer = lax.rem(date + off, n_date)
        cols = pl.ds(pl.multiple_of(peer * cols_own, cols_own), cols_own)
        copy = remote(
            x_v.at[:, cols], xcols.at[off], xcol_send.at[off], xcol_recv.at[off], (dp, peer)
        )
        copy.start()
        x_copies.append(copy)
        sent.append(copy)
    loads[7].wait()
    back = dot(stack[:tokens, :], w_v[...], 1, 1)
    dates = tokens // (patches * n_date)
    for j in range(n_date):
        pieces = [
            back[d * n_date * patches + j * patches : d * n_date * patches + (j + 1) * patches]
            for d in range(dates)
        ]
        back_send[j] = jnp.concatenate(pieces, axis=0).astype(bf16)
    for off in range(1, n_date):
        peer = lax.rem(date + off, n_date)
        copy = remote(
            back_send.at[peer], back_recv.at[off], ig_send.at[off], ig_recv.at[off], (dp, peer)
        )
        copy.start()
        ig_copies.append(copy)
        sent.append(copy)

    total = half_tile(dp, date)[...]
    for o, copy in zip(same_core, reduce_copies):
        copy.wait_recv()
        total = total + proj_recv[slot(o)]
    mine = proj_tile(dp, date)
    mine[...] = total
    for o in proj_to:
        n = slot(o)
        copy = remote(mine, mine, pg_send.at[n], pg_recv.at[n], target(o))
        copy.start()
        sent.append(copy)

    xcol = x_v[:, own_cols]
    merged[...] = stack[tokens:, :].astype(f32) + dot(xcol, stack[:tokens, :], 0, 0) * scale

    for o in proj_to:
        n = slot(o)
        source = (lax.rem(dp - o[0] + n_dp, n_dp), lax.rem(date - o[1] + n_date, n_date))
        tile = proj_tile(*source)
        remote(tile, tile, pg_send.at[n], pg_recv.at[n], target(o)).wait_recv()
    if proj_to is same_core:
        blocks = proj_full.at[my_blocks]
        copy = remote(blocks, blocks, swap_send.at[1], swap_recv.at[1], (dp, mate))
        copy.start()
        sent.append(copy)
        blocks = proj_full.at[mate_blocks]
        remote(blocks, blocks, swap_send.at[1], swap_recv.at[1], (dp, mate)).wait_recv()
    copy = slope_copy(1, 1)
    copy.start()
    sent.append(copy)
    proj_t = jnp.concatenate(
        [proj_full[j % 2 * chips + j // 2] for j in range(n_date)], axis=1
    )
    p_all = whiten(proj_t)
    p_full[...] = p_all
    p_own = p_full[:, own_cols]
    stores = [pltpu.make_async_copy(p_full.at[:, own_cols], p_out, store_sem.at[0])]
    stores[0].start()
    p_high, p_low = parts(p_all)
    z = (dot(p_high, x, 1, 1) + dot(p_low, x, 1, 1)) * scale
    left_high, left_low = parts(jnp.concatenate([z, p_own], axis=1))
    right = dot(left_high, both, 1, 0) + dot(left_low, both, 1, 0)
    right_all[...] = right
    right_send[...] = right.astype(bf16)
    my_rows = pl.ds(pl.multiple_of(core * (rank // 2), rank // 2), rank // 2)
    mate_rows = pl.ds(pl.multiple_of((1 - core) * (rank // 2), rank // 2), rank // 2)
    swap = remote(
        right_send.at[mate_rows], right_swap, swap_send.at[2], swap_recv.at[2], (dp, mate)
    )
    swap.start()
    sent.append(swap)
    swap.wait_recv()
    right_sum[...] = right_all[my_rows, :] + right_swap[...].astype(f32)
    right_half[...] = right_sum[...].astype(bf16)

    def right_tile(ref, i, j):
        return ref.at[
            pl.ds(pl.multiple_of(j * qb, qb), qb), pl.ds(pl.multiple_of(i * qa, qa), qa)
        ]

    reduce_copies = []
    for o in same_core:
        n = slot(o)
        to = target(o)
        tile = right_tile(right_half, to[0], lax.div(to[1], 2))
        copy = remote(
            tile, right_recv.at[n], qr_send.at[n], qr_recv.at[n], to
        )
        copy.start()
        reduce_copies.append(copy)
        sent.append(copy)

    for c in range(2):
        slope_copy(c, 1).wait_recv()
        copy = slope_copy(c, 2)
        copy.start()
        sent.append(copy)
    for copy in x_copies:
        copy.wait_recv()

    def add_peer(kind, peer):
        off = lax.rem(date - peer + n_date, n_date)
        return dot(xcols[off], slopes[kind], 0, 0) * scale

    for c in range(2):
        slope_copy(c, 0).wait_recv()
    merged[...] += add_peer(0, mate) + add_peer(1, across)

    total = right_tile(right_sum, dp, lax.div(date, 2))[...]
    for o, copy in zip(same_core, reduce_copies):
        copy.wait_recv()
        total = total + right_recv[slot(o)].astype(f32)
    mine = right_tile(right_full, dp, place(date))
    mine[...] = (total * (1.0 / n_dp)).astype(bf16)
    for o in right_to:
        n = slot(o)
        copy = remote(mine, mine, qg_send.at[n], qg_recv.at[n], target(o))
        copy.start()
        sent.append(copy)

    ig_rows = back_send.shape[1]
    for off, copy in zip(range(1, n_date), ig_copies):
        copy.wait_recv()
        source = lax.rem(date - off + n_date, n_date)
        ig_ref[pl.ds(pl.multiple_of(source * ig_rows, ig_rows), ig_rows), :] = back_recv[off]
    ig_ref[pl.ds(pl.multiple_of(date * ig_rows, ig_rows), ig_rows), :] = back_send[date]
    for c in range(2):
        slope_copy(c, 2).wait_recv()
    merged[...] += add_peer(2, diag)
    stores.append(pltpu.make_async_copy(ig_ref, ig_out, store_sem.at[1]))
    stores.append(pltpu.make_async_copy(merged, merged_out, store_sem.at[2]))
    stores[1].start()
    stores[2].start()

    for o in right_to:
        n = slot(o)
        source = (lax.rem(dp - o[0] + n_dp, n_dp), lax.rem(date - o[1] + n_date, n_date))
        tile = right_tile(right_full, source[0], place(source[1]))
        remote(tile, tile, qg_send.at[n], qg_recv.at[n], target(o)).wait_recv()
    if right_to is same_core:
        rows = right_full.at[my_rows]
        copy = remote(rows, rows, swap_send.at[3], swap_recv.at[3], (dp, mate))
        copy.start()
        sent.append(copy)
        rows = right_full.at[mate_rows]
        remote(rows, rows, swap_send.at[3], swap_recv.at[3], (dp, mate)).wait_recv()
    stores.append(pltpu.make_async_copy(right_full, qn_out, store_sem.at[3]))
    stores[3].start()
    for copy in stores:
        copy.wait()
    for copy in sent:
        copy.wait_send()


def finish(
    ig_hbm, p_hbm, q_hbm, merged_hbm, ig_out, p_out, q_out, eo_out, ig_v, p_v, q_v, wide_v,
    merged_v, eo_v, load_sem, store_sem
):
    rows = merged_v.shape[0] // 4
    cuts = [pl.ds(c * rows, rows) for c in range(4)]
    pairs = [(p_hbm, p_v), (q_hbm, q_v)]
    pairs += [(merged_hbm.at[cut], merged_v.at[cut]) for cut in cuts]
    pairs += [(ig_hbm, ig_v)]
    loads = [pltpu.make_async_copy(s, d, load_sem.at[n]) for n, (s, d) in enumerate(pairs)]
    for copy in loads:
        copy.start()
    pairs = [(p_v, p_out), (wide_v, q_out)]
    pairs += [(eo_v.at[cut], eo_out.at[cut]) for cut in cuts]
    pairs += [(ig_v, ig_out)]
    stores = [pltpu.make_async_copy(s, d, store_sem.at[n]) for n, (s, d) in enumerate(pairs)]
    loads[0].wait()
    stores[0].start()
    loads[1].wait()
    wide_v[...] = q_v[...].astype(f32)
    stores[1].start()
    p_high, p_low = parts(p_v[...])
    for c, cut in enumerate(cuts):
        loads[2 + c].wait()
        p_rows = slice(c * rows, (c + 1) * rows)
        low_rank = dot(p_high[:, p_rows], q_v[...], 0, 0) + dot(p_low[:, p_rows], q_v[...], 0, 0)
        eo_v[cut, :] = (merged_v[cut, :] - low_rank).astype(bf16)
        stores[2 + c].start()
    loads[6].wait()
    stores[6].start()
    for copy in stores:
        copy.wait()


def fused(n_dp, n_date, inputs, pre_act, hidden_grad, weight_in, error_in, q_prev):
    width_in, width_hidden = weight_in.shape
    rank = q_prev.shape[1]
    x = inputs.reshape(-1, width_in)
    tokens = x.shape[0]
    n = n_dp * n_date
    cols_own = width_in // n_date
    patches = inputs.shape[2] // n_date
    ig_rows = inputs.shape[1] * patches
    hbm_spec = pl.BlockSpec(memory_space=pltpu.HBM)
    dma = pltpu.SemaphoreType.DMA
    qa, qb = width_hidden // n_dp, rank // n_date
    ig, p_t, q_t, merged = pl.pallas_call(
        functools.partial(kernel, n_dp, n_date, patches),
        out_shape=(
            jax.ShapeDtypeStruct((n_date * ig_rows, width_in), bf16),
            jax.ShapeDtypeStruct((rank, cols_own), f32),
            jax.ShapeDtypeStruct((rank, width_hidden), bf16),
            jax.ShapeDtypeStruct((cols_own, width_hidden), f32),
        ),
        in_specs=[hbm_spec] * 6,
        out_specs=(hbm_spec,) * 4,
        scratch_shapes=[
            pltpu.VMEM((tokens, width_in), bf16),
            pltpu.VMEM((tokens, width_hidden), bf16),
            pltpu.VMEM((tokens, width_hidden), bf16),
            pltpu.VMEM((width_in, width_hidden), bf16),
            pltpu.VMEM((tokens + cols_own, width_hidden), bf16),
            pltpu.VMEM((rank, width_hidden), f32),
            pltpu.VMEM((3, tokens, width_hidden), bf16),
            pltpu.VMEM((n_date, tokens, cols_own), bf16),
            pltpu.VMEM((n_date, ig_rows, width_in), bf16),
            pltpu.VMEM((n_date, ig_rows, width_in), bf16),
            pltpu.VMEM((n_date, rank, cols_own), f32),
            pltpu.VMEM((n, rank // n_dp, cols_own), f32),
            pltpu.VMEM((n_date, rank, cols_own), f32),
            pltpu.VMEM((rank, width_in), f32),
            pltpu.VMEM((rank, width_hidden), bf16),
            pltpu.VMEM((n, qb, qa), bf16),
            pltpu.VMEM((rank, width_hidden), bf16),
            pltpu.VMEM((cols_own, width_hidden), f32),
            pltpu.VMEM((n_date * ig_rows, width_in), bf16),
            pltpu.VMEM((n_date // 2, rank, cols_own), f32),
            pltpu.VMEM((n_date // 2, rank, cols_own), f32),
            pltpu.VMEM((rank, width_hidden), f32),
            pltpu.VMEM((rank // 2, width_hidden), bf16),
            pltpu.VMEM((rank // 2, width_hidden), f32),
            pltpu.VMEM((rank // 2, width_hidden), bf16),
            dma((8,)),
            dma((4,)),
            dma((4,)),
            dma((4,)),
            dma((6,)),
            dma((6,)),
            dma((n_date,)),
            dma((n_date,)),
            dma((n_date,)),
            dma((n_date,)),
        ]
        + [dma((n,))] * 8,
        compiler_params=pltpu.CompilerParams(
            collective_id=0, has_side_effects=True, vmem_limit_bytes=64 * 1024 * 1024
        ),
    )(
        x,
        pre_act.reshape(tokens, width_hidden),
        hidden_grad.reshape(tokens, width_hidden),
        weight_in,
        error_in[0],
        q_prev.T,
    )
    ig, p_t, q_t, error_out = pl.pallas_call(
        finish,
        out_shape=(
            jax.ShapeDtypeStruct(ig.shape, bf16),
            jax.ShapeDtypeStruct(p_t.shape, f32),
            jax.ShapeDtypeStruct(q_t.shape, f32),
            jax.ShapeDtypeStruct(merged.shape, bf16),
        ),
        in_specs=[hbm_spec] * 4,
        out_specs=(hbm_spec,) * 4,
        scratch_shapes=[
            pltpu.VMEM(ig.shape, bf16),
            pltpu.VMEM(p_t.shape, f32),
            pltpu.VMEM(q_t.shape, bf16),
            pltpu.VMEM(q_t.shape, f32),
            pltpu.VMEM(merged.shape, f32),
            pltpu.VMEM(merged.shape, bf16),
            dma((7,)),
            dma((7,)),
        ],
        compiler_params=pltpu.CompilerParams(vmem_limit_bytes=64 * 1024 * 1024),
    )(ig, p_t, q_t, merged)
    input_grad = ig.reshape(1, -1, patches, width_in)
    return (input_grad, p_t.T, q_t.T, error_out[None])


def orthonormal(proj, gram_matrix):
    factor = jnp.linalg.cholesky(gram_matrix)
    return jax.scipy.linalg.solve_triangular(factor, proj.T, lower=True).T


def staged(inputs, pre_act, hidden_grad, weight_in, error_in, q_prev):
    date_count = lax.axis_size("date")
    width_in = inputs.shape[-1]
    width_hidden = pre_act.shape[-1]
    token_rows = inputs.reshape(-1, width_in)
    grad_scale = (token_rows.shape[0] * date_count) ** (-0.5)
    slope_grad = (
        hidden_grad.reshape(-1, width_hidden).astype(jnp.float32)
        * gelu_slope(pre_act.reshape(-1, width_hidden))
    ).astype(jnp.bfloat16)
    local_back = lax.dot_general(
        slope_grad, weight_in, (((1,), (1,)), ((), ())), preferred_element_type=jnp.float32
    ).astype(jnp.bfloat16)
    input_grad = lax.all_to_all(
        local_back.reshape(inputs.shape), "date", split_axis=2, concat_axis=1, tiled=True
    )
    column_block = lax.all_to_all(token_rows, "date", split_axis=1, concat_axis=0, tiled=True)
    own_grad = grad_scale * lax.dot_general(
        column_block,
        lax.all_gather(slope_grad, "date", axis=0, tiled=True),
        (((0,), (0,)), ((), ())),
        preferred_element_type=jnp.float32,
    )
    own_error = error_in[0].astype(jnp.float32)
    merged_rows = own_error + own_grad
    proj_rows = lax.psum(jnp.dot(merged_rows, q_prev, precision=highest), "dp")
    gram_matrix = lax.psum(jnp.dot(proj_rows.T, proj_rows, precision=highest), "date")
    p_rows = orthonormal(proj_rows, gram_matrix)
    right_part = jnp.dot(merged_rows.T, p_rows, precision=highest)
    q_new = lax.psum(right_part, ("dp", "date")) / lax.axis_size("dp")
    error_out = (merged_rows - jnp.dot(p_rows, q_new.T, precision=highest)).astype(jnp.bfloat16)[
        None
    ]
    return (input_grad, p_rows, q_new, error_out)


def solution(mesh):
    in_specs = (
        P("dp", "date", None, None),
        P("dp", "date", None, None),
        P("dp", "date", None, None),
        P(),
        P("dp", "date", None),
        P(),
    )
    out_specs = (P("dp", None, "date", None), P("date", None), P(), P("dp", "date", None))
    n_dp, n_date = mesh.shape["dp"], mesh.shape["date"]

    def local(*args):
        width_in, width_hidden = args[3].shape
        rank = args[5].shape[1]
        direct = (
            n_date == 4
            and n_dp * n_date <= 64
            and args[0].shape[0] == 1
            and rank % (8 * n_dp) == 0
            and rank % (16 * n_date) == 0
            and width_in % (128 * n_date) == 0
            and width_hidden % (128 * n_dp) == 0
            and args[0].shape[2] % (8 * n_date) == 0
        )
        if direct:
            return fused(n_dp, n_date, *args)
        return staged(*args)

    return jax.shard_map(local, mesh=mesh, in_specs=in_specs, out_specs=out_specs, check_vma=False)
```

```python
import functools

import jax
import jax.numpy as jnp
from jax import lax
from jax.experimental import pallas as pl
from jax.experimental.pallas import tpu as pltpu
from jax.sharding import PartitionSpec as P

panel = 8
inv_root2 = 0.7071067811865476
inv_root_twopi = 0.3989422804014327
highest = lax.Precision.HIGHEST
MESH = pl.DeviceIdType.MESH
f32 = jnp.float32
bf16 = jnp.bfloat16


def gelu_slope(pre_act):
    value = pre_act.astype(jnp.float32)
    return (
        0.5 * (1.0 + lax.erf(value * inv_root2))
        + value * jnp.exp(-0.5 * value * value) * inv_root_twopi
    )


def dot(a, b, ca, cb, precision=None):
    return lax.dot_general(
        a, b, (((ca,), (cb,)), ((), ())), preferred_element_type=f32, precision=precision
    )


def parts(value):
    high = value.astype(bf16)
    return high, (value - high.astype(f32)).astype(bf16)


def whiten(proj_t):
    rank = proj_t.shape[0]
    gram = dot(proj_t, proj_t, 1, 1, highest)
    rows = lax.broadcasted_iota(jnp.int32, (rank, rank), 0)
    cols = lax.broadcasted_iota(jnp.int32, (rank, rank), 1)
    eye = (rows == cols).astype(f32)
    table = jnp.concatenate([gram, eye], axis=1)
    blocks = [table[8 * i : 8 * i + 8] for i in range(rank // 8)]
    sub = lax.broadcasted_iota(jnp.int32, (8, 2 * rank), 0)
    for k in range(0, rank, panel):
        i = k // 8
        cols = {
            j: [jnp.broadcast_to(blocks[j][:, k + m : k + m + 1], sub.shape) for m in range(panel)]
            for j in range(i, rank // 8)
        }
        for m in range(panel):
            r = (k + m) % 8
            row = blocks[i][r : r + 1, :]
            inverse = 1.0 / cols[i][m][r : r + 1, :]
            heads = [cols[i][n][r : r + 1, :] for n in range(panel)]
            for j in range(i, rank // 8):
                factor = cols[j][m] * inverse
                if j == i:
                    factor = jnp.where(sub > r, factor, 0.0)
                for n in range(m + 1, panel):
                    cols[j][n] = cols[j][n] - factor * heads[n]
                blocks[j] = blocks[j] - factor * row
    table = jnp.concatenate(blocks, axis=0)
    pivots = jnp.sum(table[:, :rank] * eye, axis=1, keepdims=True)
    return dot(table[:, rank:] * lax.rsqrt(pivots), proj_t, 1, 0, highest)


def kernel(
    n_dp,
    n_date,
    patches,
    x_hbm,
    pre_hbm,
    hid_hbm,
    w_hbm,
    err_hbm,
    q_hbm,
    ig_out,
    p_out,
    qn_out,
    merged_out,
    x_v,
    pre_v,
    hid_v,
    w_v,
    stack,
    q_v,
    slopes,
    xcols,
    back_send,
    back_recv,
    proj_part,
    proj_recv,
    proj_full,
    p_full,
    right_send,
    right_recv,
    right_full,
    merged,
    ig_ref,
    proj_swap,
    proj_half,
    right_all,
    right_swap,
    right_sum,
    right_half,
    load_sem,
    store_sem,
    swap_send,
    swap_recv,
    slope_send,
    slope_recv,
    xcol_send,
    xcol_recv,
    ig_send,
    ig_recv,
    pr_send,
    pr_recv,
    pg_send,
    pg_recv,
    qr_send,
    qr_recv,
    qg_send,
    qg_recv,
):
    tokens, width_in = x_v.shape
    width_hidden = stack.shape[1]
    rank = q_v.shape[0]
    cols_own = width_in // n_date
    scale = (tokens * n_date) ** (-0.5)
    pa = rank // n_dp
    qa, qb = width_hidden // n_dp, rank // n_date
    half = tokens // 2
    dp = lax.axis_index("dp")
    date = lax.axis_index("date")
    others = [(i, j) for i in range(n_dp) for j in range(n_date) if i + j > 0]
    others = sorted(others, key=lambda o: -min(o[0], n_dp - o[0]))
    same_core = [o for o in others if o[1] % 2 == 0]
    proj_to = others
    right_to = same_core
    core = lax.rem(date, 2)
    chips = n_date // 2

    def place(j):
        return lax.rem(j, 2) * chips + lax.div(j, 2)

    def slot(o):
        return o[0] * n_date + o[1]

    def target(o):
        return lax.rem(dp + o[0], n_dp), lax.rem(date + o[1], n_date)

    loads = []
    for c in range(2):
        for h, v in ((pre_hbm, pre_v), (hid_hbm, hid_v)):
            rows = pl.ds(c * half, half)
            loads.append((h.at[rows], v.at[rows]))
    loads.append((q_hbm, q_v))
    loads.append((err_hbm, stack.at[pl.ds(tokens, cols_own)]))
    loads.append((x_hbm, x_v))
    loads.append((w_hbm, w_v))
    loads = [pltpu.make_async_copy(s, d, load_sem.at[n]) for n, (s, d) in enumerate(loads)]
    for copy in loads:
        copy.start()

    barrier = pltpu.get_barrier_semaphore()
    for o in others:
        pl.semaphore_signal(barrier, inc=1, device_id=target(o), device_id_type=MESH)

    def remote(src, dst, send, recv, device):
        return pltpu.make_async_remote_copy(
            src_ref=src,
            dst_ref=dst,
            send_sem=send,
            recv_sem=recv,
            device_id=device,
            device_id_type=MESH,
        )

    mate = date + 1 - 2 * lax.rem(date, 2)
    across = lax.rem(date + 2, n_date)
    diag = lax.rem(mate + 2, n_date)
    sent = []

    def slope_copy(c, kind):
        rows = pl.ds(c * half, half)
        src = stack.at[rows] if kind < 2 else slopes.at[1, rows]
        device = (dp, across if kind == 1 else mate)
        n = 2 * kind + c
        return remote(src, slopes.at[kind, rows], slope_send.at[n], slope_recv.at[n], device)

    for c in range(2):
        loads[2 * c].wait()
        loads[2 * c + 1].wait()
        for s in range(half // 16):
            rows = pl.ds(c * half + s * 16, 16)
            stack[rows, :] = (hid_v[rows, :].astype(f32) * gelu_slope(pre_v[rows, :])).astype(bf16)
        if c == 0:
            pl.semaphore_wait(barrier, len(others))
        for kind in (1, 0) if c == 0 else (0,):
            copy = slope_copy(c, kind)
            copy.start()
            sent.append(copy)

    loads[4].wait()
    loads[5].wait()
    q_high, q_low = parts(q_v[...])
    both = stack[...]
    seen = dot(q_high, both, 1, 1) + dot(q_low, both, 1, 1)
    loads[6].wait()
    x = x_v[...]
    y_high, y_low = parts(seen[:, :tokens] * scale)
    part = dot(y_high, x, 1, 0) + dot(y_low, x, 1, 0)
    for j in range(n_date):
        proj_part[j % 2 * chips + j // 2] = part[:, j * cols_own : (j + 1) * cols_own]
    proj_part[place(date)] += seen[:, tokens:]

    own_cols = pl.ds(pl.multiple_of(date * cols_own, cols_own), cols_own)
    my_blocks = pl.ds(core * chips, chips)
    mate_blocks = pl.ds((1 - core) * chips, chips)
    swap = remote(
        proj_part.at[mate_blocks], proj_swap, swap_send.at[0], swap_recv.at[0], (dp, mate)
    )
    swap.start()
    sent.append(swap)
    swap.wait_recv()
    proj_half[...] = proj_part[my_blocks] + proj_swap[...]

    def proj_rows(i):
        return pl.ds(pl.multiple_of(i * pa, pa), pa)

    def half_tile(i, j):
        return proj_half.at[lax.div(j, 2), proj_rows(i)]

    def proj_tile(i, j):
        return proj_full.at[place(j), proj_rows(i)]

    reduce_copies = []
    for o in same_core:
        n = slot(o)
        to = target(o)
        copy = remote(half_tile(*to), proj_recv.at[n], pr_send.at[n], pr_recv.at[n], to)
        copy.start()
        reduce_copies.append(copy)
        sent.append(copy)

    x_copies, ig_copies = [], []
    for off in range(1, n_date):
        peer = lax.rem(date + off, n_date)
        cols = pl.ds(pl.multiple_of(peer * cols_own, cols_own), cols_own)
        copy = remote(
            x_v.at[:, cols], xcols.at[off], xcol_send.at[off], xcol_recv.at[off], (dp, peer)
        )
        copy.start()
        x_copies.append(copy)
        sent.append(copy)
    loads[7].wait()
    back = dot(stack[:tokens, :], w_v[...], 1, 1)
    dates = tokens // (patches * n_date)
    for j in range(n_date):
        pieces = [
            back[d * n_date * patches + j * patches : d * n_date * patches + (j + 1) * patches]
            for d in range(dates)
        ]
        back_send[j] = jnp.concatenate(pieces, axis=0).astype(bf16)
    for off in range(1, n_date):
        peer = lax.rem(date + off, n_date)
        copy = remote(
            back_send.at[peer], back_recv.at[off], ig_send.at[off], ig_recv.at[off], (dp, peer)
        )
        copy.start()
        ig_copies.append(copy)
        sent.append(copy)

    total = half_tile(dp, date)[...]
    for o, copy in zip(same_core, reduce_copies):
        copy.wait_recv()
        total = total + proj_recv[slot(o)]
    mine = proj_tile(dp, date)
    mine[...] = total
    for o in proj_to:
        n = slot(o)
        copy = remote(mine, mine, pg_send.at[n], pg_recv.at[n], target(o))
        copy.start()
        sent.append(copy)

    xcol = x_v[:, own_cols]
    merged[...] = stack[tokens:, :].astype(f32) + dot(xcol, stack[:tokens, :], 0, 0) * scale

    for o in proj_to:
        n = slot(o)
        source = (lax.rem(dp - o[0] + n_dp, n_dp), lax.rem(date - o[1] + n_date, n_date))
        tile = proj_tile(*source)
        remote(tile, tile, pg_send.at[n], pg_recv.at[n], target(o)).wait_recv()
    if proj_to is same_core:
        blocks = proj_full.at[my_blocks]
        copy = remote(blocks, blocks, swap_send.at[1], swap_recv.at[1], (dp, mate))
        copy.start()
        sent.append(copy)
        blocks = proj_full.at[mate_blocks]
        remote(blocks, blocks, swap_send.at[1], swap_recv.at[1], (dp, mate)).wait_recv()
    copy = slope_copy(1, 1)
    copy.start()
    sent.append(copy)
    proj_t = jnp.concatenate(
        [proj_full[j % 2 * chips + j // 2] for j in range(n_date)], axis=1
    )
    p_all = whiten(proj_t)
    p_full[...] = p_all
    p_own = p_full[:, own_cols]
    stores = [pltpu.make_async_copy(p_full.at[:, own_cols], p_out, store_sem.at[0])]
    stores[0].start()
    p_high, p_low = parts(p_all)
    z = (dot(p_high, x, 1, 1) + dot(p_low, x, 1, 1)) * scale
    left_high, left_low = parts(jnp.concatenate([z, p_own], axis=1))
    right = dot(left_high, both, 1, 0) + dot(left_low, both, 1, 0)
    right_all[...] = right
    right_send[...] = right.astype(bf16)
    my_rows = pl.ds(pl.multiple_of(core * (rank // 2), rank // 2), rank // 2)
    mate_rows = pl.ds(pl.multiple_of((1 - core) * (rank // 2), rank // 2), rank // 2)
    swap = remote(
        right_send.at[mate_rows], right_swap, swap_send.at[2], swap_recv.at[2], (dp, mate)
    )
    swap.start()
    sent.append(swap)
    swap.wait_recv()
    right_sum[...] = right_all[my_rows, :] + right_swap[...].astype(f32)
    right_half[...] = right_sum[...].astype(bf16)

    def right_tile(ref, i, j):
        return ref.at[
            pl.ds(pl.multiple_of(j * qb, qb), qb), pl.ds(pl.multiple_of(i * qa, qa), qa)
        ]

    reduce_copies = []
    for o in same_core:
        n = slot(o)
        to = target(o)
        tile = right_tile(right_half, to[0], lax.div(to[1], 2))
        copy = remote(
            tile, right_recv.at[n], qr_send.at[n], qr_recv.at[n], to
        )
        copy.start()
        reduce_copies.append(copy)
        sent.append(copy)

    total = right_tile(right_sum, dp, lax.div(date, 2))[...]
    for o, copy in zip(same_core, reduce_copies):
        copy.wait_recv()
        total = total + right_recv[slot(o)].astype(f32)
    mine = right_tile(right_full, dp, place(date))
    mine[...] = (total * (1.0 / n_dp)).astype(bf16)
    for o in right_to:
        n = slot(o)
        copy = remote(mine, mine, qg_send.at[n], qg_recv.at[n], target(o))
        copy.start()
        sent.append(copy)

    for c in range(2):
        slope_copy(c, 1).wait_recv()
        copy = slope_copy(c, 2)
        copy.start()
        sent.append(copy)
    for copy in x_copies:
        copy.wait_recv()

    def add_peer(kind, peer):
        off = lax.rem(date - peer + n_date, n_date)
        return dot(xcols[off], slopes[kind], 0, 0) * scale

    for c in range(2):
        slope_copy(c, 0).wait_recv()
    merged[...] += add_peer(0, mate) + add_peer(1, across)

    ig_rows = back_send.shape[1]
    for off, copy in zip(range(1, n_date), ig_copies):
        copy.wait_recv()
        source = lax.rem(date - off + n_date, n_date)
        ig_ref[pl.ds(pl.multiple_of(source * ig_rows, ig_rows), ig_rows), :] = back_recv[off]
    ig_ref[pl.ds(pl.multiple_of(date * ig_rows, ig_rows), ig_rows), :] = back_send[date]
    for c in range(2):
        slope_copy(c, 2).wait_recv()
    merged[...] += add_peer(2, diag)
    stores.append(pltpu.make_async_copy(ig_ref, ig_out, store_sem.at[1]))
    stores.append(pltpu.make_async_copy(merged, merged_out, store_sem.at[2]))
    stores[1].start()
    stores[2].start()

    for o in right_to:
        n = slot(o)
        source = (lax.rem(dp - o[0] + n_dp, n_dp), lax.rem(date - o[1] + n_date, n_date))
        tile = right_tile(right_full, source[0], place(source[1]))
        remote(tile, tile, qg_send.at[n], qg_recv.at[n], target(o)).wait_recv()
    if right_to is same_core:
        rows = right_full.at[my_rows]
        copy = remote(rows, rows, swap_send.at[3], swap_recv.at[3], (dp, mate))
        copy.start()
        sent.append(copy)
        rows = right_full.at[mate_rows]
        remote(rows, rows, swap_send.at[3], swap_recv.at[3], (dp, mate)).wait_recv()
    stores.append(pltpu.make_async_copy(right_full, qn_out, store_sem.at[3]))
    stores[3].start()
    for copy in stores:
        copy.wait()
    for copy in sent:
        copy.wait_send()


def finish(
    ig_hbm, p_hbm, q_hbm, merged_hbm, ig_out, p_out, q_out, eo_out, ig_v, p_v, q_v, wide_v,
    merged_v, eo_v, load_sem, store_sem
):
    rows = merged_v.shape[0] // 4
    cuts = [pl.ds(c * rows, rows) for c in range(4)]
    pairs = [(p_hbm, p_v), (q_hbm, q_v)]
    pairs += [(merged_hbm.at[cut], merged_v.at[cut]) for cut in cuts]
    pairs += [(ig_hbm, ig_v)]
    loads = [pltpu.make_async_copy(s, d, load_sem.at[n]) for n, (s, d) in enumerate(pairs)]
    for copy in loads:
        copy.start()
    pairs = [(p_v, p_out), (wide_v, q_out)]
    pairs += [(eo_v.at[cut], eo_out.at[cut]) for cut in cuts]
    pairs += [(ig_v, ig_out)]
    stores = [pltpu.make_async_copy(s, d, store_sem.at[n]) for n, (s, d) in enumerate(pairs)]
    loads[0].wait()
    stores[0].start()
    loads[1].wait()
    wide_v[...] = q_v[...].astype(f32)
    stores[1].start()
    p_high, p_low = parts(p_v[...])
    for c, cut in enumerate(cuts):
        loads[2 + c].wait()
        p_rows = slice(c * rows, (c + 1) * rows)
        low_rank = dot(p_high[:, p_rows], q_v[...], 0, 0) + dot(p_low[:, p_rows], q_v[...], 0, 0)
        eo_v[cut, :] = (merged_v[cut, :] - low_rank).astype(bf16)
        stores[2 + c].start()
    loads[6].wait()
    stores[6].start()
    for copy in stores:
        copy.wait()


def fused(n_dp, n_date, inputs, pre_act, hidden_grad, weight_in, error_in, q_prev):
    width_in, width_hidden = weight_in.shape
    rank = q_prev.shape[1]
    x = inputs.reshape(-1, width_in)
    tokens = x.shape[0]
    n = n_dp * n_date
    cols_own = width_in // n_date
    patches = inputs.shape[2] // n_date
    ig_rows = inputs.shape[1] * patches
    hbm_spec = pl.BlockSpec(memory_space=pltpu.HBM)
    dma = pltpu.SemaphoreType.DMA
    qa, qb = width_hidden // n_dp, rank // n_date
    ig, p_t, q_t, merged = pl.pallas_call(
        functools.partial(kernel, n_dp, n_date, patches),
        out_shape=(
            jax.ShapeDtypeStruct((n_date * ig_rows, width_in), bf16),
            jax.ShapeDtypeStruct((rank, cols_own), f32),
            jax.ShapeDtypeStruct((rank, width_hidden), bf16),
            jax.ShapeDtypeStruct((cols_own, width_hidden), f32),
        ),
        in_specs=[hbm_spec] * 6,
        out_specs=(hbm_spec,) * 4,
        scratch_shapes=[
            pltpu.VMEM((tokens, width_in), bf16),
            pltpu.VMEM((tokens, width_hidden), bf16),
            pltpu.VMEM((tokens, width_hidden), bf16),
            pltpu.VMEM((width_in, width_hidden), bf16),
            pltpu.VMEM((tokens + cols_own, width_hidden), bf16),
            pltpu.VMEM((rank, width_hidden), f32),
            pltpu.VMEM((3, tokens, width_hidden), bf16),
            pltpu.VMEM((n_date, tokens, cols_own), bf16),
            pltpu.VMEM((n_date, ig_rows, width_in), bf16),
            pltpu.VMEM((n_date, ig_rows, width_in), bf16),
            pltpu.VMEM((n_date, rank, cols_own), f32),
            pltpu.VMEM((n, rank // n_dp, cols_own), f32),
            pltpu.VMEM((n_date, rank, cols_own), f32),
            pltpu.VMEM((rank, width_in), f32),
            pltpu.VMEM((rank, width_hidden), bf16),
            pltpu.VMEM((n, qb, qa), bf16),
            pltpu.VMEM((rank, width_hidden), bf16),
            pltpu.VMEM((cols_own, width_hidden), f32),
            pltpu.VMEM((n_date * ig_rows, width_in), bf16),
            pltpu.VMEM((n_date // 2, rank, cols_own), f32),
            pltpu.VMEM((n_date // 2, rank, cols_own), f32),
            pltpu.VMEM((rank, width_hidden), f32),
            pltpu.VMEM((rank // 2, width_hidden), bf16),
            pltpu.VMEM((rank // 2, width_hidden), f32),
            pltpu.VMEM((rank // 2, width_hidden), bf16),
            dma((8,)),
            dma((4,)),
            dma((4,)),
            dma((4,)),
            dma((6,)),
            dma((6,)),
            dma((n_date,)),
            dma((n_date,)),
            dma((n_date,)),
            dma((n_date,)),
        ]
        + [dma((n,))] * 8,
        compiler_params=pltpu.CompilerParams(
            collective_id=0, has_side_effects=True, vmem_limit_bytes=64 * 1024 * 1024
        ),
    )(
        x,
        pre_act.reshape(tokens, width_hidden),
        hidden_grad.reshape(tokens, width_hidden),
        weight_in,
        error_in[0],
        q_prev.T,
    )
    ig, p_t, q_t, error_out = pl.pallas_call(
        finish,
        out_shape=(
            jax.ShapeDtypeStruct(ig.shape, bf16),
            jax.ShapeDtypeStruct(p_t.shape, f32),
            jax.ShapeDtypeStruct(q_t.shape, f32),
            jax.ShapeDtypeStruct(merged.shape, bf16),
        ),
        in_specs=[hbm_spec] * 4,
        out_specs=(hbm_spec,) * 4,
        scratch_shapes=[
            pltpu.VMEM(ig.shape, bf16),
            pltpu.VMEM(p_t.shape, f32),
            pltpu.VMEM(q_t.shape, bf16),
            pltpu.VMEM(q_t.shape, f32),
            pltpu.VMEM(merged.shape, f32),
            pltpu.VMEM(merged.shape, bf16),
            dma((7,)),
            dma((7,)),
        ],
        compiler_params=pltpu.CompilerParams(vmem_limit_bytes=64 * 1024 * 1024),
    )(ig, p_t, q_t, merged)
    input_grad = ig.reshape(1, -1, patches, width_in)
    return (input_grad, p_t.T, q_t.T, error_out[None])


def orthonormal(proj, gram_matrix):
    factor = jnp.linalg.cholesky(gram_matrix)
    return jax.scipy.linalg.solve_triangular(factor, proj.T, lower=True).T


def staged(inputs, pre_act, hidden_grad, weight_in, error_in, q_prev):
    date_count = lax.axis_size("date")
    width_in = inputs.shape[-1]
    width_hidden = pre_act.shape[-1]
    token_rows = inputs.reshape(-1, width_in)
    grad_scale = (token_rows.shape[0] * date_count) ** (-0.5)
    slope_grad = (
        hidden_grad.reshape(-1, width_hidden).astype(jnp.float32)
        * gelu_slope(pre_act.reshape(-1, width_hidden))
    ).astype(jnp.bfloat16)
    local_back = lax.dot_general(
        slope_grad, weight_in, (((1,), (1,)), ((), ())), preferred_element_type=jnp.float32
    ).astype(jnp.bfloat16)
    input_grad = lax.all_to_all(
        local_back.reshape(inputs.shape), "date", split_axis=2, concat_axis=1, tiled=True
    )
    column_block = lax.all_to_all(token_rows, "date", split_axis=1, concat_axis=0, tiled=True)
    own_grad = grad_scale * lax.dot_general(
        column_block,
        lax.all_gather(slope_grad, "date", axis=0, tiled=True),
        (((0,), (0,)), ((), ())),
        preferred_element_type=jnp.float32,
    )
    own_error = error_in[0].astype(jnp.float32)
    merged_rows = own_error + own_grad
    proj_rows = lax.psum(jnp.dot(merged_rows, q_prev, precision=highest), "dp")
    gram_matrix = lax.psum(jnp.dot(proj_rows.T, proj_rows, precision=highest), "date")
    p_rows = orthonormal(proj_rows, gram_matrix)
    right_part = jnp.dot(merged_rows.T, p_rows, precision=highest)
    q_new = lax.psum(right_part, ("dp", "date")) / lax.axis_size("dp")
    error_out = (merged_rows - jnp.dot(p_rows, q_new.T, precision=highest)).astype(jnp.bfloat16)[
        None
    ]
    return (input_grad, p_rows, q_new, error_out)


def solution(mesh):
    in_specs = (
        P("dp", "date", None, None),
        P("dp", "date", None, None),
        P("dp", "date", None, None),
        P(),
        P("dp", "date", None),
        P(),
    )
    out_specs = (P("dp", None, "date", None), P("date", None), P(), P("dp", "date", None))
    n_dp, n_date = mesh.shape["dp"], mesh.shape["date"]

    def local(*args):
        width_in, width_hidden = args[3].shape
        rank = args[5].shape[1]
        direct = (
            n_date == 4
            and n_dp * n_date <= 64
            and args[0].shape[0] == 1
            and rank % (8 * n_dp) == 0
            and rank % (16 * n_date) == 0
            and width_in % (128 * n_date) == 0
            and width_hidden % (128 * n_dp) == 0
            and args[0].shape[2] % (8 * n_date) == 0
        )
        if direct:
            return fused(n_dp, n_date, *args)
        return staged(*args)

    return jax.shard_map(local, mesh=mesh, in_specs=in_specs, out_specs=out_specs, check_vma=False)
```
